32 devices in a mesh: parts: 2 (over x), img: 8 (over z, y), vol: 2 (over core).
Axes of the slice: x: 2, y: 2, z: 4, core: 2. Of those that a mesh axis runs over, the one named last changes fastest.
Arguments:
- images: bfloat16 [256, 256, 256], P(('parts', 'img', 'vol')), parts along dimension 0, may hold values from -6 to 6
- pose_index: int32 [256], P(('parts', 'img', 'vol')), parts along dimension 0, may hold values from 0 to 127
- ctf_index: int32 [256], P(('parts', 'img', 'vol')), parts along dimension 0, may hold values from 0 to 3
- crossing: int32 [256, 64], P(('parts', 'img', 'vol')), parts along dimension 0, may hold values from 0 to 7
- volume: bfloat16 [16, 32, 2, 1024], P(('parts', 'vol')), parts along dimension 0, may hold values from -6 to 6
- pose_table: float32 [128, 64, 32], replicated, may hold values from -1 to 1
- ctf_table: float32 [4, 64, 1024], replicated, may hold values from -1 to 1
Outputs:
- brick_gradient: float32 [16, 32, 2, 1024], P(('parts', 'vol')), parts along dimension 0
The draws below stay inside these ranges and needn't reach their ends.
There are 2 independent parts, one for each index of `parts`. The reference program is written for one: setup_inputs(seed, part) draws one part's arguments, and reference() takes and returns one part's arrays. A program takes and returns all parts, laid end to end along the dimension named above; an argument that names none is the same for every part. Nothing has to cross between parts.
All inputs are finite; a program needn't handle non-finite values.
Results may differ from the reference program's by a relative error of at most 0.0018.
Values may be sent and summed in bfloat16 or wider, within the bound.
A program may use at most 128 MiB of HBM per device.

```python
import math
import jax
import jax.numpy as jnp
from jax import lax

SIDE = 256
BRICK = 32
TILES = 64
CELLS = 1024
NPOSE = 128
NCTF = 4
NIMG = 128
NB = 8


def with_ends(entries, key, low, top_value):
    longest = entries.shape.index(max(entries.shape))
    spots = []
    for shift in (0, 1):
        where = [jax.random.randint(jax.random.fold_in(key, axis), (), 0, length) for axis, length in enumerate(entries.shape)]
        where[longest] = (where[longest] + shift) % entries.shape[longest]
        spots.append(tuple(where))
    return entries.at[spots[0]].set(low).at[spots[1]].set(top_value)


def block_levels(own_key, extent, pieces, low, largest):
    level, own = 1.0, jax.random.fold_in(own_key, 6)
    for dim, shards_of in pieces:
        draws = jnp.exp(jax.random.uniform(jax.random.fold_in(own, dim), (shards_of,), jnp.float32, low / len(pieces), largest / len(pieces)))
        level = level * jnp.repeat(draws, extent[dim] // shards_of).reshape([-1 if axis == dim else 1 for axis in range(len(extent))])
    return level


def centred(rng, extent, deviation, bound, pieces=(), held_as=jnp.bfloat16):
    entries = deviation * jax.random.normal(rng, extent, jnp.float32)
    if pieces:
        entries = entries * block_levels(rng, extent, pieces, -0.22, 0.18)
    return jnp.clip(entries, -bound, bound).astype(held_as)


def setup_inputs(seed: int = 0, part: int = 0) -> dict:
    arg_keys = jax.random.split(jax.random.key(seed), 8)
    part_splits = jax.random.split(jax.random.fold_in(arg_keys[7], part), 8)
    images = centred(part_splits[0], (NIMG, SIDE, SIDE), 1.0, 6.0, ((0, 16),))
    pose_index = with_ends(jax.random.randint(part_splits[1], (NIMG,), 0, NPOSE), jax.random.fold_in(part_splits[1], 1), 0, NPOSE - 1).astype(jnp.int32)
    ctf_index = with_ends(jax.random.randint(part_splits[2], (NIMG,), 0, NCTF), jax.random.fold_in(part_splits[2], 1), 0, NCTF - 1).astype(jnp.int32)
    crossing = with_ends(jax.random.randint(part_splits[3], (NIMG, TILES), 0, NB), jax.random.fold_in(part_splits[3], 1), 0, NB - 1).astype(jnp.int32)
    volume = centred(part_splits[4], (NB, BRICK, 2, CELLS), 1.0, 6.0, ((0, 2),))
    pose_table = centred(arg_keys[5], (NPOSE, TILES, BRICK), BRICK ** -0.5, 1.0, (), jnp.float32)
    ctf_table = jnp.clip(jax.random.uniform(arg_keys[6], (NCTF, TILES, CELLS), jnp.float32, -1.0, 1.0), -1.0, 1.0)
    return dict(images=images, pose_index=pose_index, ctf_index=ctf_index, crossing=crossing, volume=volume, pose_table=pose_table, ctf_table=ctf_table)


def dft_tables(image_side):
    position = jnp.arange(image_side, dtype=jnp.int32)
    product = position[:, None] * position[None, :] % image_side
    angles = product.astype(jnp.float32) * (2.0 * math.pi / image_side)
    table_scale = 1.0 / math.sqrt(image_side)
    return ((jnp.cos(angles) * table_scale).astype(jnp.bfloat16), (jnp.sin(angles) * table_scale).astype(jnp.bfloat16))

def reference(images, pose_index, ctf_index, crossing, volume, pose_table, ctf_table):
    cosine_table, sine_table = dft_tables(SIDE)
    cos_full = cosine_table.astype(jnp.float32)
    sin_full = sine_table.astype(jnp.float32)
    tile_rows = SIDE // BRICK
    block_images = 8
    tile_total = block_images * TILES
    volume_flat = volume.astype(jnp.float32).reshape(NB * BRICK, 2 * CELLS)
    brick_ids = jnp.arange(NB, dtype=jnp.int32)

    def one_block(carry, block):
        pixels, poses, transfer_ids, crossed = block
        pixels = pixels.astype(jnp.float32)
        half_cos = jnp.einsum('nxy,yv->nxv', pixels, cos_full)
        half_sin = jnp.einsum('nxy,yv->nxv', pixels, sin_full)
        half_cos = lax.optimization_barrier(half_cos.astype(jnp.bfloat16)).astype(jnp.float32)
        half_sin = lax.optimization_barrier(half_sin.astype(jnp.bfloat16)).astype(jnp.float32)
        real_part = jnp.einsum('ux,nxv->nuv', cos_full, half_cos) - jnp.einsum('ux,nxv->nuv', sin_full, half_sin)
        imag_part = -(jnp.einsum('ux,nxv->nuv', cos_full, half_sin) + jnp.einsum('ux,nxv->nuv', sin_full, half_cos))
        spectra = jnp.stack([real_part, imag_part], axis=1)
        spectra = lax.optimization_barrier(spectra.astype(jnp.bfloat16)).astype(jnp.float32)
        tiled_spec = spectra.reshape(block_images, 2, tile_rows, BRICK, tile_rows, BRICK)
        tiled_spec = tiled_spec.transpose(0, 2, 4, 1, 3, 5).reshape(tile_total, 2, CELLS)
        weights = lax.optimization_barrier(pose_table[poses].astype(jnp.bfloat16)).astype(jnp.float32)
        onehot = (crossed[:, :, None] == brick_ids[None, None, :]).astype(jnp.float32)
        weight_full = (onehot[:, :, :, None] * weights[:, :, None, :]).reshape(tile_total, NB * BRICK)
        slices = jnp.dot(weight_full, volume_flat, precision=lax.Precision.HIGHEST)
        transfer = ctf_table[transfer_ids].reshape(tile_total, 1, CELLS).astype(jnp.float32)
        misfit = transfer * slices.reshape(tile_total, 2, CELLS) - tiled_spec
        back_term = lax.optimization_barrier((transfer * misfit).astype(jnp.bfloat16)).astype(jnp.float32)
        grad_part = jnp.dot(weight_full.T, back_term.reshape(tile_total, 2 * CELLS), precision=lax.Precision.HIGHEST)
        return (carry + grad_part, None)
    blocks = (images.reshape(NIMG // block_images, block_images, SIDE, SIDE), pose_index.reshape(NIMG // block_images, block_images), ctf_index.reshape(NIMG // block_images, block_images), crossing.reshape(NIMG // block_images, block_images, TILES))
    final, _ = lax.scan(one_block, jnp.zeros((NB * BRICK, 2 * CELLS), jnp.float32), blocks)
    grad_scale = 2.0 * math.sqrt(BRICK * NB / (NIMG * TILES))
    return (final * grad_scale).reshape(NB, BRICK, 2, CELLS)
```

```python
import functools
import math

import jax
import jax.numpy as jnp
import numpy as np
from jax import lax
from jax.experimental import pallas as pl
from jax.experimental.pallas import tpu as pltpu
from jax.sharding import PartitionSpec as P

MESH = pl.DeviceIdType.MESH
LN2 = math.log(2.0)


def dft_tables(side, tile_rows):
    position = np.arange(side, dtype=np.int32)
    product = position[:, None] * position[None, :] % side
    angles = product.astype(np.float32) * np.float32(2.0 * math.pi / side)
    scale = np.float32(1.0 / math.sqrt(side))
    cosine = np.cos(angles) * scale
    sine = np.sin(angles) * scale
    first = np.concatenate([cosine, sine], axis=1)
    order = position.reshape(tile_rows, side // tile_rows).T.reshape(-1)
    cos_rows, sin_rows = cosine[order], sine[order]
    second = np.concatenate(
        [
            np.concatenate([cos_rows, -sin_rows], axis=1),
            np.concatenate([-sin_rows, -cos_rows], axis=1),
        ],
        axis=0,
    )
    return first.astype(jnp.bfloat16), second.astype(jnp.bfloat16)


def block_transpose(parts, lane):
    low = lane < 64
    odd = (lane // 32) % 2 == 1
    x0, x1, x2, x3 = parts
    a0 = jnp.where(low, x0, pltpu.roll(x2, 64, 1))
    a2 = jnp.where(low, pltpu.roll(x0, 64, 1), x2)
    a1 = jnp.where(low, x1, pltpu.roll(x3, 64, 1))
    a3 = jnp.where(low, pltpu.roll(x1, 64, 1), x3)
    y0 = jnp.where(odd, pltpu.roll(a1, 32, 1), a0)
    y1 = jnp.where(odd, a1, pltpu.roll(a0, 96, 1))
    y2 = jnp.where(odd, pltpu.roll(a3, 32, 1), a2)
    y3 = jnp.where(odd, a3, pltpu.roll(a2, 96, 1))
    return y0, y1, y2, y3


def spectrum_kernel(image_ref, first_ref, second_ref, tiles_ref):
    side = image_ref.shape[1]
    half = jnp.dot(image_ref[0], first_ref[...], preferred_element_type=jnp.float32)
    half = half.astype(jnp.bfloat16)
    half = jnp.concatenate([half[:, :side], half[:, side:]], axis=0)
    spec = jnp.dot(second_ref[...], half, preferred_element_type=jnp.float32)
    groups = spec.shape[0] // 32
    spec = spec.reshape(groups, 4, 8, side)
    lane = lax.broadcasted_iota(jnp.int32, (groups * 8, 128), 1)
    for group in range(side // 128):
        parts = [
            spec[:, low, :, group * 128 : (group + 1) * 128].reshape(groups * 8, 128)
            for low in range(4)
        ]
        done = [y.reshape(groups, 8, 128) for y in block_transpose(parts, lane)]
        for pair in range(2):
            both = jnp.concatenate([done[2 * pair], done[2 * pair + 1]], axis=1)
            both = both.astype(jnp.bfloat16)
            row = group * 32 + pair * 16
            for g in range(groups):
                tiles_ref[row : row + 16, g * 128 : (g + 1) * 128] = both[g]


def gradient_kernel(
    scale, pose_ref, ctf_index_ref, crossing_ref, ctf_ref, pose_table_ref, tiles_ref,
    volume_ref, grads_ref, weight_ref, weight_t_ref, transfer_ref, pose_rows_ref, sem,
):
    step = pl.program_id(0)
    image_count = pose_rows_ref.shape[0]
    tile_rows = 8
    columns = volume_ref.shape[1]
    cells = transfer_ref.shape[1]

    @pl.when(step == 0)
    def _():
        for n in range(image_count):
            pltpu.make_async_copy(
                pose_table_ref.at[pose_ref[n]], pose_rows_ref.at[n], sem.at[n]
            ).start()
        for n in range(image_count):
            rows = ctf_ref[ctf_index_ref[n]].reshape(tile_rows, 8, cells)
            transfer_ref[n * tile_rows * 8 : (n + 1) * tile_rows * 8, :] = jnp.swapaxes(
                rows, 0, 1
            ).reshape(tile_rows * 8, cells)
        for n in range(image_count):
            pltpu.make_async_copy(
                pose_table_ref.at[pose_ref[n]], pose_rows_ref.at[n], sem.at[n]
            ).wait()
        planes = pose_rows_ref.shape[2]
        rows = [
            jnp.swapaxes(pose_rows_ref[n].reshape(tile_rows, 8, planes), 0, 1).reshape(
                tile_rows * 8, planes
            )
            for n in range(image_count)
        ]
        small = jnp.concatenate(rows, axis=0).astype(jnp.bfloat16)
        full = weight_ref.shape[1]
        spread = (
            lax.broadcasted_iota(jnp.int32, (planes, full), 1) % planes
            == lax.broadcasted_iota(jnp.int32, (planes, full), 0)
        ).astype(jnp.bfloat16)
        wide = jnp.dot(small, spread, preferred_element_type=jnp.float32)
        brick = lax.broadcasted_iota(jnp.int32, wide.shape, 1) // planes
        wide = jnp.where(brick == crossing_ref[...], wide, 0.0)
        weight_ref[...] = wide.astype(jnp.bfloat16)
        weight_t_ref[...] = wide.T.astype(jnp.bfloat16)

    start = pl.multiple_of((step % (cells // columns)) * columns, columns)
    transfer = transfer_ref[:, pl.ds(start, columns)]
    slices = jnp.dot(weight_ref[...], volume_ref[...], preferred_element_type=jnp.float32)
    misfit = transfer * slices - tiles_ref[...].astype(jnp.float32)
    back = (transfer * misfit).astype(jnp.bfloat16)
    grads_ref[...] = scale * jnp.dot(
        weight_t_ref[...], back, preferred_element_type=jnp.float32
    )


def encode(values, out_ref):
    width = values.shape[1]
    top = jnp.max(jnp.abs(values), axis=1, keepdims=True)
    exponent = jnp.ceil(jnp.log(jnp.maximum(top, 1e-30)) * (1.0 / LN2))
    codes = jnp.floor(values * jnp.exp((14.0 - exponent) * LN2) + 0.5)
    out_ref[:, :width] = codes.astype(jnp.int32).astype(jnp.int16)
    spread = jnp.broadcast_to(exponent, (values.shape[0], 128))
    out_ref[:, width:] = spread.astype(jnp.int32).astype(jnp.int16)


def decode(in_ref):
    width = in_ref.shape[1] - 128
    exponent = in_ref[:, width:].astype(jnp.int32).astype(jnp.float32)
    factor = jnp.exp((exponent - 14.0) * LN2)[:, :1]
    return in_ref[:, :width].astype(jnp.int32).astype(jnp.float32) * factor


def reduce_kernel(
    peers, col_blocks, grads_ref, out_ref, other_ref, send_ref, recv_ref, total_ref,
    gather_ref, core_send, core_recv, rs_send, rs_recv, ag_send, ag_recv,
):
    me = lax.axis_index("img")
    core = lax.axis_index("vol")
    owner_rows, width = out_ref.shape
    chunk_rows = owner_rows // (peers // col_blocks)
    chunk_cols = width // col_blocks

    def place(chunk):
        row = pl.multiple_of((chunk // col_blocks) * chunk_rows, 16)
        col = pl.multiple_of((chunk % col_blocks) * chunk_cols, 128)
        return row, col

    barrier = pltpu.get_barrier_semaphore()
    pl.semaphore_signal(barrier, inc=1, device_id={"vol": 1 - core}, device_id_type=MESH)

    def greet(step, carry):
        pl.semaphore_signal(
            barrier, inc=1, device_id={"img": lax.rem(me + step, peers)}, device_id_type=MESH
        )
        return carry

    lax.fori_loop(1, peers, greet, 0)
    pl.semaphore_wait(barrier, peers)

    def core_copy(chunk):
        row, col = place(chunk)
        there = pl.multiple_of((1 - core) * owner_rows, 16) + row
        return pltpu.make_async_remote_copy(
            src_ref=grads_ref.at[pl.ds(there, chunk_rows), pl.ds(col, chunk_cols)],
            dst_ref=other_ref.at[pl.ds(row, chunk_rows), pl.ds(col, chunk_cols)],
            send_sem=core_send.at[chunk],
            recv_sem=core_recv.at[chunk],
            device_id={"vol": 1 - core},
            device_id_type=MESH,
        )

    def rs_copy(target, slot):
        return pltpu.make_async_remote_copy(
            src_ref=send_ref.at[target],
            dst_ref=recv_ref.at[slot],
            send_sem=rs_send.at[target],
            recv_sem=rs_recv.at[slot],
            device_id={"img": target},
            device_id_type=MESH,
        )

    def ag_copy(target, slot):
        return pltpu.make_async_remote_copy(
            src_ref=gather_ref.at[slot],
            dst_ref=gather_ref.at[slot],
            send_sem=ag_send.at[target],
            recv_sem=ag_recv.at[slot],
            device_id={"img": target},
            device_id_type=MESH,
        )

    def core_start(step, carry):
        core_copy(lax.rem(me + step, peers)).start()
        return carry

    lax.fori_loop(1, peers + 1, core_start, 0)

    def chip_sum(chunk):
        core_copy(chunk).wait_recv()
        row, col = place(chunk)
        here = pl.multiple_of(core * owner_rows, 16) + row
        return (
            grads_ref[pl.ds(here, chunk_rows), pl.ds(col, chunk_cols)]
            + other_ref[pl.ds(row, chunk_rows), pl.ds(col, chunk_cols)]
        )

    def scatter(step, carry):
        target = lax.rem(me + step, peers)
        encode(chip_sum(target), send_ref.at[target])
        rs_copy(target, me).start()
        return carry

    lax.fori_loop(1, peers, scatter, 0)
    total_ref[...] = chip_sum(me)

    def collect(step, carry):
        source = lax.rem(me + peers - step, peers)
        rs_copy(source, source).wait_recv()
        total_ref[...] += decode(recv_ref.at[source])
        return carry

    lax.fori_loop(1, peers, collect, 0)
    encode(total_ref[...], gather_ref.at[me])

    def spread(step, carry):
        ag_copy(lax.rem(me + step, peers), me).start()
        return carry

    lax.fori_loop(1, peers, spread, 0)

    def write(source):
        row, col = place(source)
        out_ref[pl.ds(row, chunk_rows), pl.ds(col, chunk_cols)] = decode(gather_ref.at[source])

    write(me)

    def finish(step, carry):
        source = lax.rem(me + peers - step, peers)
        ag_copy(source, source).wait_recv()
        write(source)
        return carry

    lax.fori_loop(1, peers, finish, 0)

    def drain(step, carry):
        target = lax.rem(me + step, peers)
        rs_copy(target, me).wait_send()
        ag_copy(target, me).wait_send()
        return carry

    lax.fori_loop(1, peers, drain, 0)

    def drain_core(chunk, carry):
        core_copy(chunk).wait_send()
        return carry

    lax.fori_loop(0, peers, drain_core, 0)


def on_device(images, pose_index, ctf_index, crossing, volume, pose_table, ctf_table):
    image_count, side, _ = images.shape
    owned, planes, parts, cells = volume.shape
    tile_rows = side // planes
    tile_count = tile_rows * tile_rows
    owners = lax.axis_size("vol")
    peers = lax.axis_size("img")
    bricks = owned * owners
    rows = image_count * tile_count
    width = parts * cells
    weight_rows = bricks * planes
    total_images = image_count * peers * owners
    grad_scale = 2.0 * math.sqrt(planes * bricks / (total_images * tile_count))
    first, second = dft_tables(side, tile_rows)

    received = lax.all_gather(volume.reshape(owned * planes, width), "vol", axis=0, tiled=True)
    tiles = pl.pallas_call(
        spectrum_kernel,
        grid=(image_count,),
        out_shape=jax.ShapeDtypeStruct((rows, width), jnp.bfloat16),
        in_specs=[
            pl.BlockSpec((1, side, side), lambda n: (n, 0, 0)),
            pl.BlockSpec((side, 2 * side), lambda n: (0, 0)),
            pl.BlockSpec((2 * side, 2 * side), lambda n: (0, 0)),
        ],
        out_specs=pl.BlockSpec((tile_count, width), lambda n: (n, 0)),
        compiler_params=pltpu.CompilerParams(vmem_limit_bytes=32 * 2**20),
        cost_estimate=pl.CostEstimate(
            flops=image_count * 12 * side**3, bytes_accessed=4 * 2**20, transcendentals=0
        ),
    )(images, jnp.asarray(first), jnp.asarray(second))

    crossed = crossing.reshape(image_count, tile_rows, tile_rows)
    crossed = crossed.transpose(0, 2, 1).reshape(rows, 1)
    columns = 256
    grads = pl.pallas_call(
        functools.partial(gradient_kernel, grad_scale),
        grid=(width // columns,),
        out_shape=jax.ShapeDtypeStruct((weight_rows, width), jnp.float32),
        in_specs=[
            pl.BlockSpec(memory_space=pltpu.SMEM),
            pl.BlockSpec(memory_space=pltpu.SMEM),
            pl.BlockSpec((rows, 1), lambda s: (0, 0)),
            pl.BlockSpec(ctf_table.shape, lambda s: (0, 0, 0)),
            pl.BlockSpec(memory_space=pl.ANY),
            pl.BlockSpec((rows, columns), lambda s: (0, s)),
            pl.BlockSpec((weight_rows, columns), lambda s: (0, s)),
        ],
        out_specs=pl.BlockSpec((weight_rows, columns), lambda s: (0, s)),
        scratch_shapes=[
            pltpu.VMEM((rows, weight_rows), jnp.bfloat16),
            pltpu.VMEM((weight_rows, rows), jnp.bfloat16),
            pltpu.VMEM((rows, cells), jnp.float32),
            pltpu.VMEM((image_count, tile_count, planes), jnp.float32),
            pltpu.SemaphoreType.DMA((image_count,)),
        ],
        compiler_params=pltpu.CompilerParams(vmem_limit_bytes=32 * 2**20),
        cost_estimate=pl.CostEstimate(
            flops=4 * rows * weight_rows * width, bytes_accessed=8 * 2**20, transcendentals=0
        ),
    )(pose_index, ctf_index, crossed, ctf_table, pose_table, tiles, received)

    owner_rows = owned * planes
    col_blocks = max(1, peers // (owner_rows // 16))
    chunk = (owner_rows // (peers // col_blocks), width // col_blocks)
    code = (peers, chunk[0], chunk[1] + 128)
    summed = pl.pallas_call(
        functools.partial(reduce_kernel, peers, col_blocks),
        out_shape=jax.ShapeDtypeStruct((owner_rows, width), jnp.float32),
        in_specs=[pl.BlockSpec(memory_space=pltpu.VMEM)],
        out_specs=pl.BlockSpec(memory_space=pltpu.VMEM),
        scratch_shapes=[
            pltpu.VMEM((owner_rows, width), jnp.float32),
            pltpu.VMEM(code, jnp.int16),
            pltpu.VMEM(code, jnp.int16),
            pltpu.VMEM(chunk, jnp.float32),
            pltpu.VMEM(code, jnp.int16),
        ]
        + [pltpu.SemaphoreType.DMA((peers,))] * 6,
        compiler_params=pltpu.CompilerParams(
            collective_id=0, has_side_effects=True, vmem_limit_bytes=32 * 2**20
        ),
        cost_estimate=pl.CostEstimate(
            flops=2**20, bytes_accessed=4 * 2**20, transcendentals=0
        ),
    )(grads)
    return summed.reshape(owned, planes, parts, cells)


def solution(mesh):
    in_specs = (
        P(("parts", "img", "vol"), None, None),
        P(("parts", "img", "vol")),
        P(("parts", "img", "vol")),
        P(("parts", "img", "vol"), None),
        P(("parts", "vol"), None, None, None),
        P(),
        P(),
    )
    out_specs = P(("parts", "vol"), None, None, None)
    return jax.shard_map(
        on_device, mesh=mesh, in_specs=in_specs, out_specs=out_specs, check_vma=False
    )
```

```python
import functools
import math

import jax
import jax.numpy as jnp
import numpy as np
from jax import lax
from jax.experimental import pallas as pl
from jax.experimental.pallas import tpu as pltpu
from jax.sharding import PartitionSpec as P

MESH = pl.DeviceIdType.MESH
LN2 = math.log(2.0)


def dft_tables(side, tile_rows):
    position = np.arange(side, dtype=np.int32)
    product = position[:, None] * position[None, :] % side
    angles = product.astype(np.float32) * np.float32(2.0 * math.pi / side)
    scale = np.float32(1.0 / math.sqrt(side))
    cosine = np.cos(angles) * scale
    sine = np.sin(angles) * scale
    first = np.concatenate([cosine, sine], axis=1)
    order = position.reshape(tile_rows, side // tile_rows).T.reshape(-1)
    cos_rows, sin_rows = cosine[order], sine[order]
    second = np.concatenate(
        [
            np.concatenate([cos_rows, -sin_rows], axis=1),
            np.concatenate([-sin_rows, -cos_rows], axis=1),
        ],
        axis=0,
    )
    return first.astype(jnp.bfloat16), second.astype(jnp.bfloat16)


def block_transpose(parts, lane):
    low = lane < 64
    odd = (lane // 32) % 2 == 1
    x0, x1, x2, x3 = parts
    a0 = jnp.where(low, x0, pltpu.roll(x2, 64, 1))
    a2 = jnp.where(low, pltpu.roll(x0, 64, 1), x2)
    a1 = jnp.where(low, x1, pltpu.roll(x3, 64, 1))
    a3 = jnp.where(low, pltpu.roll(x1, 64, 1), x3)
    y0 = jnp.where(odd, pltpu.roll(a1, 32, 1), a0)
    y1 = jnp.where(odd, a1, pltpu.roll(a0, 96, 1))
    y2 = jnp.where(odd, pltpu.roll(a3, 32, 1), a2)
    y3 = jnp.where(odd, a3, pltpu.roll(a2, 96, 1))
    return y0, y1, y2, y3


def spectrum_kernel(image_ref, first_ref, second_ref, tiles_ref):
    side = image_ref.shape[1]
    half = jnp.dot(image_ref[0], first_ref[...], preferred_element_type=jnp.float32)
    half = half.astype(jnp.bfloat16)
    half = jnp.concatenate([half[:, :side], half[:, side:]], axis=0)
    spec = jnp.dot(second_ref[...], half, preferred_element_type=jnp.float32)
    groups = spec.shape[0] // 32
    spec = spec.reshape(groups, 4, 8, side)
    lane = lax.broadcasted_iota(jnp.int32, (groups * 8, 128), 1)
    for group in range(side // 128):
        parts = [
            spec[:, low, :, group * 128 : (group + 1) * 128].reshape(groups * 8, 128)
            for low in range(4)
        ]
        done = [y.reshape(groups, 8, 128) for y in block_transpose(parts, lane)]
        for pair in range(2):
            both = jnp.concatenate([done[2 * pair], done[2 * pair + 1]], axis=1)
            both = both.astype(jnp.bfloat16)
            row = group * 32 + pair * 16
            for g in range(groups):
                tiles_ref[row : row + 16, g * 128 : (g + 1) * 128] = both[g]


def encode(values, out_ref):
    height, width = values.shape
    top = jnp.max(jnp.abs(values), axis=1, keepdims=True)
    peak = top[:16]
    for row in range(16, height, 16):
        peak = jnp.maximum(peak, top[row : row + 16])
    exponent = jnp.ceil(jnp.log(jnp.maximum(peak, 1e-30)) * (1.0 / LN2))
    factor = jnp.broadcast_to(jnp.exp((14.0 - exponent) * LN2), (16, 128))
    for col in range(0, width, 128):
        for row in range(0, height, 16):
            block = values[row : row + 16, col : col + 128]
            codes = jnp.floor(block * factor + 0.5).astype(jnp.int32).astype(jnp.int16)
            place = (col // 128) * height + row
            out_ref[place : place + 16, :] = codes
    spread = jnp.broadcast_to(exponent, (16, 128)).astype(jnp.int32).astype(jnp.int16)
    out_ref[height * (width // 128) :, :] = spread


def decode(in_ref, height):
    total = in_ref.shape[0] - 16
    exponent = in_ref[total:, :].astype(jnp.int32).astype(jnp.float32)
    factor = jnp.exp((exponent - 14.0) * LN2)
    columns = []
    for base in range(0, total, height):
        rows = [
            in_ref[base + row : base + row + 16, :].astype(jnp.int32).astype(jnp.float32) * factor
            for row in range(0, height, 16)
        ]
        columns.append(jnp.concatenate(rows, axis=0))
    return jnp.concatenate(columns, axis=1)


def gradient_kernel(
    scale, pieces, outer, col_blocks,
    ctf_index_ref, crossing_ref, pose_rows_ref, ctf_ref, tiles_ref, volume_ref, out_ref,
    ctf_buf, tiles_buf, volume_buf, weight_ref, weight_t_ref, transfer_ref,
    grads_ref, other_ref, pair_out, pair_in, half_ref, send_ref, recv_ref, total_ref,
    gather_ref, pair_gather, load_sem, core_send, core_recv, pair_send, pair_recv,
    rs_send, rs_recv, ag_send, ag_recv, fw_send, fw_recv,
):
    img = lax.axis_index("img")
    core = lax.axis_index("vol")
    me = img // 2
    side = img - 2 * me
    pair_device = 2 * me + 1 - side
    owner_rows, width = out_ref.shape
    half_rows = owner_rows // 2
    cells = transfer_ref.shape[1]
    columns = width // pieces
    chunk_cols = columns // col_blocks

    loads = [
        pltpu.make_async_copy(source, target, load_sem.at[k])
        for k, (source, target) in enumerate(
            [(ctf_ref, ctf_buf), (volume_ref, volume_buf), (tiles_ref, tiles_buf)]
        )
    ]
    for load in loads:
        load.start()

    barrier = pltpu.get_barrier_semaphore()
    pl.semaphore_signal(barrier, inc=1, device_id={"vol": 1 - core}, device_id_type=MESH)
    pl.semaphore_signal(barrier, inc=1, device_id={"img": pair_device}, device_id_type=MESH)

    def peer(step):
        return lax.rem(me + step, outer)

    def greet(step, carry):
        pl.semaphore_signal(
            barrier, inc=1, device_id={"img": 2 * peer(step) + side}, device_id_type=MESH
        )
        return carry

    lax.fori_loop(1, outer, greet, 0)

    planes = pose_rows_ref.shape[1]
    full = weight_ref.shape[1]
    spread = (
        lax.broadcasted_iota(jnp.int32, (planes, full), 1) % planes
        == lax.broadcasted_iota(jnp.int32, (planes, full), 0)
    ).astype(jnp.bfloat16)
    wide = jnp.dot(pose_rows_ref[...], spread, preferred_element_type=jnp.float32)
    brick = lax.broadcasted_iota(jnp.int32, wide.shape, 1) // planes
    wide = jnp.where(brick == crossing_ref[...], wide, 0.0)
    weight_ref[...] = wide.astype(jnp.bfloat16)
    weight_t_ref[...] = wide.T.astype(jnp.bfloat16)

    loads[0].wait()
    tile_count = ctf_buf.shape[1]
    tile_rows = tile_count // 8
    for n in range(weight_ref.shape[0] // tile_count):
        rows = ctf_buf[ctf_index_ref[n]].reshape(tile_rows, 8, cells)
        transfer_ref[n * tile_count : (n + 1) * tile_count, :] = jnp.swapaxes(
            rows, 0, 1
        ).reshape(tile_count, cells)
    loads[1].wait()
    loads[2].wait()
    pl.semaphore_wait(barrier, outer + 1)

    def remote(source, target, send, recv, device):
        return pltpu.make_async_remote_copy(
            src_ref=source, dst_ref=target, send_sem=send, recv_sem=recv,
            device_id=device, device_id_type=MESH,
        )

    def core_copy(p):
        there = pl.multiple_of((1 - core) * owner_rows, 16)
        return remote(
            grads_ref.at[p, pl.ds(there, owner_rows), :], other_ref.at[p],
            core_send.at[p], core_recv.at[p], {"vol": 1 - core},
        )

    def pair_copy(p):
        return remote(
            pair_out.at[p], pair_in.at[p], pair_send.at[p], pair_recv.at[p],
            {"img": pair_device},
        )

    def rs_copy(p, target, slot):
        return remote(
            send_ref.at[p, target], recv_ref.at[p, slot],
            rs_send.at[p, target], rs_recv.at[p, slot], {"img": 2 * target + side},
        )

    def ag_copy(p, target, slot):
        return remote(
            gather_ref.at[p, slot], gather_ref.at[p, slot],
            ag_send.at[p, target], ag_recv.at[p, slot], {"img": 2 * target + side},
        )

    def fw_copy(p, slot):
        return remote(
            gather_ref.at[p, slot], pair_gather.at[p, slot],
            fw_send.at[p, slot], fw_recv.at[p, slot], {"img": pair_device},
        )

    def place(chunk):
        row = pl.multiple_of((chunk // col_blocks) * 16, 16)
        col = pl.multiple_of((chunk % col_blocks) * chunk_cols, 128)
        return pl.ds(row, 16), pl.ds(col, chunk_cols)

    def write(p, chunk, which, codes_ref):
        row = pl.multiple_of((chunk // col_blocks) * 16 + which * half_rows, 16)
        col = pl.multiple_of((chunk % col_blocks) * chunk_cols + p * columns, 128)
        out_ref[pl.ds(row, 16), pl.ds(col, chunk_cols)] = decode(codes_ref, 16)

    def compute(p):
        start = p * columns
        transfer = transfer_ref[:, start % cells : start % cells + columns]
        slices = jnp.dot(
            weight_ref[...], volume_buf[:, start : start + columns],
            preferred_element_type=jnp.float32,
        )
        tiles = tiles_buf[:, start : start + columns].astype(jnp.float32)
        back = (transfer * (transfer * slices - tiles)).astype(jnp.bfloat16)
        grads_ref[p] = scale * jnp.dot(
            weight_t_ref[...], back, preferred_element_type=jnp.float32
        )
        core_copy(p).start()

    def to_pair(p):
        core_copy(p).wait_recv()
        mine = pl.multiple_of(side * half_rows, 16)
        his = pl.multiple_of((1 - side) * half_rows, 16)
        here = core * owner_rows
        encode(
            grads_ref[p, pl.ds(pl.multiple_of(here + his, 16), half_rows), :]
            + other_ref[p, pl.ds(his, half_rows), :],
            pair_out.at[p],
        )
        pair_copy(p).start()
        half_ref[p] = (
            grads_ref[p, pl.ds(pl.multiple_of(here + mine, 16), half_rows), :]
            + other_ref[p, pl.ds(mine, half_rows), :]
        )

    def scatter(p):
        pair_copy(p).wait_recv()
        half_ref[p] += decode(pair_in.at[p], half_rows)

        def one(step, carry):
            target = peer(step)
            rows, cols = place(target)
            encode(half_ref[p, rows, cols], send_ref.at[p, target])
            rs_copy(p, target, me).start()
            return carry

        lax.fori_loop(1, outer, one, 0)
        rows, cols = place(me)
        total_ref[p] = half_ref[p, rows, cols]

    def collect(p):
        def one(step, carry):
            source = peer(outer - step)
            rs_copy(p, source, source).wait_recv()
            total_ref[p] += decode(recv_ref.at[p, source], 16)
            return carry

        lax.fori_loop(1, outer, one, 0)
        encode(total_ref[p], gather_ref.at[p, me])

        def share(step, carry):
            ag_copy(p, peer(step), me).start()
            return carry

        lax.fori_loop(1, outer, share, 0)
        fw_copy(p, me).start()
        write(p, me, side, gather_ref.at[p, me])

    def forward(p):
        def one(step, carry):
            source = peer(outer - step)
            ag_copy(p, source, source).wait_recv()
            fw_copy(p, source).start()
            write(p, source, side, gather_ref.at[p, source])
            return carry

        lax.fori_loop(1, outer, one, 0)

    def finish(p):
        def one(step, carry):
            source = peer(outer - step)
            fw_copy(p, source).wait_recv()
            write(p, source, 1 - side, pair_gather.at[p, source])
            return carry

        lax.fori_loop(0, outer, one, 0)

    stages = [compute, to_pair, scatter, collect, forward, finish]
    for step in range(pieces + len(stages) - 1):
        for age, stage in enumerate(stages):
            if 0 <= step - age < pieces:
                stage(step - age)

    for p in range(pieces):
        core_copy(p).wait_send()
        pair_copy(p).wait_send()

        def drain(step, carry, p=p):
            target = peer(step)
            rs_copy(p, target, me).wait_send()
            ag_copy(p, target, me).wait_send()
            fw_copy(p, target).wait_send()
            return carry

        lax.fori_loop(1, outer, drain, 0)
        fw_copy(p, me).wait_send()


def on_device(images, pose_index, ctf_index, crossing, volume, pose_table, ctf_table):
    image_count, side, _ = images.shape
    owned, planes, parts, cells = volume.shape
    tile_rows = side // planes
    tile_count = tile_rows * tile_rows
    owners = lax.axis_size("vol")
    peers = lax.axis_size("img")
    bricks = owned * owners
    rows = image_count * tile_count
    width = parts * cells
    weight_rows = bricks * planes
    total_images = image_count * peers * owners
    grad_scale = 2.0 * math.sqrt(planes * bricks / (total_images * tile_count))
    first, second = dft_tables(side, tile_rows)

    received = lax.all_gather(volume.reshape(owned * planes, width), "vol", axis=0, tiled=True)
    tiles = pl.pallas_call(
        spectrum_kernel,
        grid=(image_count,),
        out_shape=jax.ShapeDtypeStruct((rows, width), jnp.bfloat16),
        in_specs=[
            pl.BlockSpec((1, side, side), lambda n: (n, 0, 0)),
            pl.BlockSpec((side, 2 * side), lambda n: (0, 0)),
            pl.BlockSpec((2 * side, 2 * side), lambda n: (0, 0)),
        ],
        out_specs=pl.BlockSpec((tile_count, width), lambda n: (n, 0)),
        compiler_params=pltpu.CompilerParams(vmem_limit_bytes=56 * 2**20),
        cost_estimate=pl.CostEstimate(
            flops=image_count * 12 * side**3, bytes_accessed=4 * 2**20, transcendentals=0
        ),
    )(images, jnp.asarray(first), jnp.asarray(second))

    crossed = crossing.reshape(image_count, tile_rows, tile_rows)
    crossed = crossed.transpose(0, 2, 1).reshape(rows, 1)
    chosen = pose_index[:, None] == lax.iota(jnp.int32, pose_table.shape[0])[None, :]
    pose_rows = jnp.einsum(
        "np,ptk->ntk", chosen.astype(jnp.bfloat16), pose_table.astype(jnp.bfloat16),
        preferred_element_type=jnp.bfloat16,
    )
    pose_rows = pose_rows.reshape(image_count, tile_rows, tile_rows, planes)
    pose_rows = pose_rows.transpose(0, 2, 1, 3).reshape(rows, planes)

    owner_rows = owned * planes
    half_rows = owner_rows // 2
    outer = peers // 2
    col_blocks = max(1, outer // (half_rows // 16))
    pieces = min(4, width // (128 * col_blocks))
    columns = width // pieces
    chunk = (16, columns // col_blocks)
    code = (pieces, outer, 16 * (chunk[1] // 128) + 16, 128)
    pair_code = (pieces, half_rows * (columns // 128) + 16, 128)
    summed = pl.pallas_call(
        functools.partial(gradient_kernel, grad_scale, pieces, outer, col_blocks),
        out_shape=jax.ShapeDtypeStruct((owner_rows, width), jnp.float32),
        in_specs=[pl.BlockSpec(memory_space=pltpu.SMEM)]
        + [pl.BlockSpec(memory_space=pltpu.VMEM)] * 2
        + [pl.BlockSpec(memory_space=pl.ANY)] * 3,
        out_specs=pl.BlockSpec(memory_space=pltpu.VMEM),
        scratch_shapes=[
            pltpu.VMEM(ctf_table.shape, jnp.float32),
            pltpu.VMEM((rows, width), jnp.bfloat16),
            pltpu.VMEM((weight_rows, width), jnp.bfloat16),
            pltpu.VMEM((rows, weight_rows), jnp.bfloat16),
            pltpu.VMEM((weight_rows, rows), jnp.bfloat16),
            pltpu.VMEM((rows, cells), jnp.float32),
            pltpu.VMEM((pieces, weight_rows, columns), jnp.float32),
            pltpu.VMEM((pieces, owner_rows, columns), jnp.float32),
            pltpu.VMEM(pair_code, jnp.int16),
            pltpu.VMEM(pair_code, jnp.int16),
            pltpu.VMEM((pieces, half_rows, columns), jnp.float32),
            pltpu.VMEM(code, jnp.int16),
            pltpu.VMEM(code, jnp.int16),
            pltpu.VMEM((pieces,) + chunk, jnp.float32),
            pltpu.VMEM(code, jnp.int16),
            pltpu.VMEM(code, jnp.int16),
            pltpu.SemaphoreType.DMA((3,)),
        ]
        + [pltpu.SemaphoreType.DMA((pieces,))] * 4
        + [pltpu.SemaphoreType.DMA((pieces, outer))] * 6,
        compiler_params=pltpu.CompilerParams(
            collective_id=0, has_side_effects=True, vmem_limit_bytes=56 * 2**20
        ),
        cost_estimate=pl.CostEstimate(
            flops=4 * rows * weight_rows * width, bytes_accessed=8 * 2**20, transcendentals=0
        ),
    )(ctf_index, crossed, pose_rows, ctf_table, tiles, received)
    return summed.reshape(owned, planes, parts, cells)


def solution(mesh):
    in_specs = (
        P(("parts", "img", "vol"), None, None),
        P(("parts", "img", "vol")),
        P(("parts", "img", "vol")),
        P(("parts", "img", "vol"), None),
        P(("parts", "vol"), None, None, None),
        P(),
        P(),
    )
    out_specs = P(("parts", "vol"), None, None, None)
    return jax.shard_map(
        on_device, mesh=mesh, in_specs=in_specs, out_specs=out_specs, check_vma=False
    )
```

```python
import functools
import math

import jax
import jax.numpy as jnp
import numpy as np
from jax import lax
from jax.experimental import pallas as pl
from jax.experimental.pallas import tpu as pltpu
from jax.sharding import PartitionSpec as P

MESH = pl.DeviceIdType.MESH
LN2 = math.log(2.0)


def dft_tables(side, tile_rows):
    position = np.arange(side, dtype=np.int32)
    product = position[:, None] * position[None, :] % side
    angles = product.astype(np.float32) * np.float32(2.0 * math.pi / side)
    scale = np.float32(1.0 / math.sqrt(side))
    cosine = np.cos(angles) * scale
    sine = np.sin(angles) * scale
    first = np.concatenate([cosine, sine], axis=1)
    order = position.reshape(tile_rows, side // tile_rows).T.reshape(-1)
    cos_rows, sin_rows = cosine[order], sine[order]
    second = np.concatenate(
        [
            np.concatenate([cos_rows, -sin_rows], axis=1),
            np.concatenate([-sin_rows, -cos_rows], axis=1),
        ],
        axis=0,
    )
    return first.astype(jnp.bfloat16), second.astype(jnp.bfloat16)


def block_transpose(parts, lane):
    low = lane < 64
    odd = (lane // 32) % 2 == 1
    x0, x1, x2, x3 = parts
    a0 = jnp.where(low, x0, pltpu.roll(x2, 64, 1))
    a2 = jnp.where(low, pltpu.roll(x0, 64, 1), x2)
    a1 = jnp.where(low, x1, pltpu.roll(x3, 64, 1))
    a3 = jnp.where(low, pltpu.roll(x1, 64, 1), x3)
    y0 = jnp.where(odd, pltpu.roll(a1, 32, 1), a0)
    y1 = jnp.where(odd, a1, pltpu.roll(a0, 96, 1))
    y2 = jnp.where(odd, pltpu.roll(a3, 32, 1), a2)
    y3 = jnp.where(odd, a3, pltpu.roll(a2, 96, 1))
    return y0, y1, y2, y3


def tile_spectrum(image, first, second, tiles_ref, start):
    side = image.shape[1]
    half = jnp.dot(image, first, preferred_element_type=jnp.float32).astype(jnp.bfloat16)
    half = jnp.concatenate([half[:, :side], half[:, side:]], axis=0)
    spec = jnp.dot(second, half, preferred_element_type=jnp.float32)
    groups = spec.shape[0] // 32
    spec = spec.reshape(groups, 4, 8, side)
    lane = lax.broadcasted_iota(jnp.int32, (groups * 8, 128), 1)
    for group in range(side // 128):
        parts = [
            spec[:, low, :, group * 128 : (group + 1) * 128].reshape(groups * 8, 128)
            for low in range(4)
        ]
        done = [y.reshape(groups, 8, 128) for y in block_transpose(parts, lane)]
        for pair in range(2):
            both = jnp.concatenate([done[2 * pair], done[2 * pair + 1]], axis=1)
            both = both.astype(jnp.bfloat16)
            rows = pl.ds(pl.multiple_of(start + group * 32 + pair * 16, 16), 16)
            for g in range(groups):
                tiles_ref[rows, g * 128 : (g + 1) * 128] = both[g]


def encode(values, out_ref):
    height, width = values.shape
    top = jnp.max(jnp.abs(values), axis=1, keepdims=True)
    peak = top[:16]
    for row in range(16, height, 16):
        peak = jnp.maximum(peak, top[row : row + 16])
    exponent = jnp.ceil(jnp.log(jnp.maximum(peak, 1e-30)) * (1.0 / LN2))
    factor = jnp.broadcast_to(jnp.exp((14.0 - exponent) * LN2), (16, 128))
    for col in range(0, width, 128):
        for row in range(0, height, 16):
            block = values[row : row + 16, col : col + 128]
            codes = jnp.floor(block * factor + 0.5).astype(jnp.int32).astype(jnp.int16)
            place = (col // 128) * height + row
            out_ref[place : place + 16, :] = codes
    spread = jnp.broadcast_to(exponent, (16, 128)).astype(jnp.int32).astype(jnp.int16)
    out_ref[height * (width // 128) :, :] = spread


def decode(in_ref, height):
    total = in_ref.shape[0] - 16
    exponent = in_ref[total:, :].astype(jnp.int32).astype(jnp.float32)
    factor = jnp.exp((exponent - 14.0) * LN2)
    columns = []
    for base in range(0, total, height):
        rows = [
            in_ref[base + row : base + row + 16, :].astype(jnp.int32).astype(jnp.float32) * factor
            for row in range(0, height, 16)
        ]
        columns.append(jnp.concatenate(rows, axis=0))
    return jnp.concatenate(columns, axis=1)


def gradient_kernel(
    scale, pieces, outer, col_blocks,
    ctf_index_ref, crossing_ref, pose_rows_ref, ctf_ref, volume_ref, image_ref, first_ref,
    second_ref, out_ref,
    ctf_buf, volume_buf, image_buf, first_buf, second_buf, tiles_buf,
    weight_ref, weight_t_ref, transfer_ref,
    grads_ref, other_ref, pair_out, pair_in, half_ref, send_ref, recv_ref, total_ref,
    gather_ref, pair_gather, load_sem, image_sem, vol_send, vol_recv, core_send, core_recv, pair_send, pair_recv,
    rs_send, rs_recv, ag_send, ag_recv, fw_send, fw_recv,
):
    img = lax.axis_index("img")
    core = lax.axis_index("vol")
    me = img // 2
    side = img - 2 * me
    pair_device = 2 * me + 1 - side
    owner_rows, width = out_ref.shape
    half_rows = owner_rows // 2
    cells = transfer_ref.shape[1]
    columns = width // pieces
    chunk_cols = columns // col_blocks

    image_count = image_buf.shape[0]
    own_bricks = volume_buf.at[core]
    loads = [
        pltpu.make_async_copy(source, target, load_sem.at[k])
        for k, (source, target) in enumerate(
            [
                (volume_ref, own_bricks),
                (first_ref, first_buf),
                (second_ref, second_buf),
                (ctf_ref, ctf_buf),
            ]
        )
    ]
    images = [
        pltpu.make_async_copy(image_ref.at[n], image_buf.at[n], image_sem.at[n])
        for n in range(image_count)
    ]
    for load in loads[:3] + images + loads[3:]:
        load.start()

    barrier = pltpu.get_barrier_semaphore()
    pl.semaphore_signal(barrier, inc=1, device_id={"vol": 1 - core}, device_id_type=MESH)
    pl.semaphore_signal(barrier, inc=1, device_id={"img": pair_device}, device_id_type=MESH)

    def peer(step):
        return lax.rem(me + step, outer)

    def greet(step, carry):
        pl.semaphore_signal(
            barrier, inc=1, device_id={"img": 2 * peer(step) + side}, device_id_type=MESH
        )
        return carry

    lax.fori_loop(1, outer, greet, 0)

    planes = pose_rows_ref.shape[1]
    tile_count = pose_rows_ref.shape[2]
    tile_rows = tile_count // 8
    full, row_count = weight_t_ref.shape
    poses = jnp.concatenate(
        [pose_rows_ref[n].astype(jnp.float32) for n in range(image_count)], axis=1
    )
    crossed = jnp.concatenate([crossing_ref[n : n + 1, :] for n in range(image_count)], axis=1)
    brick = lax.broadcasted_iota(jnp.int32, (full, row_count), 0) // planes
    wide = jnp.where(
        brick == crossed, jnp.concatenate([poses] * (full // planes), axis=0), 0.0
    ).astype(jnp.bfloat16)
    column = lax.broadcasted_iota(jnp.int32, (1, row_count), 1)
    source = (
        column // tile_count * tile_count + column % 8 * tile_rows + column % tile_count // 8
    )
    order = jnp.where(
        lax.broadcasted_iota(jnp.int32, (row_count, row_count), 0) == source, 1.0, 0.0
    ).astype(jnp.bfloat16)
    wide = jnp.dot(wide, order, preferred_element_type=jnp.float32)
    weight_t_ref[...] = wide.astype(jnp.bfloat16)
    weight_ref[...] = wide.T.astype(jnp.bfloat16)

    def remote(source, target, send, recv, device):
        return pltpu.make_async_remote_copy(
            src_ref=source, dst_ref=target, send_sem=send, recv_sem=recv,
            device_id=device, device_id_type=MESH,
        )

    volume_copy = remote(
        own_bricks, own_bricks, vol_send, vol_recv, {"vol": 1 - core}
    )
    loads[0].wait()
    pl.semaphore_wait(barrier, outer + 1)
    volume_copy.start()
    loads[1].wait()
    loads[2].wait()
    for n in range(image_count):
        images[n].wait()

    def transform(n, carry):
        start = n * tile_count
        tile_spectrum(image_buf[n], first_buf[...], second_buf[...], tiles_buf, start)
        return carry

    lax.fori_loop(0, image_count, transform, 0)
    loads[3].wait()
    for n in range(image_count):
        rows = ctf_buf[ctf_index_ref[n]].reshape(tile_rows, 8, cells)
        transfer_ref[n * tile_count : (n + 1) * tile_count, :] = jnp.swapaxes(
            rows, 0, 1
        ).reshape(tile_count, cells)
    volume_copy.wait()

    def core_copy(p):
        there = pl.multiple_of((1 - core) * owner_rows, 16)
        return remote(
            grads_ref.at[p, pl.ds(there, owner_rows), :], other_ref.at[p],
            core_send.at[p], core_recv.at[p], {"vol": 1 - core},
        )

    def pair_copy(p):
        return remote(
            pair_out.at[p], pair_in.at[p], pair_send.at[p], pair_recv.at[p],
            {"img": pair_device},
        )

    def rs_copy(p, target, slot):
        return remote(
            send_ref.at[p, target], recv_ref.at[p, slot],
            rs_send.at[p, target], rs_recv.at[p, slot], {"img": 2 * target + side},
        )

    def ag_copy(p, target, slot):
        return remote(
            gather_ref.at[p, slot], gather_ref.at[p, slot],
            ag_send.at[p, target], ag_recv.at[p, slot], {"img": 2 * target + side},
        )

    def fw_copy(p, slot):
        return remote(
            gather_ref.at[p, slot], pair_gather.at[p, slot],
            fw_send.at[p, slot], fw_recv.at[p, slot], {"img": pair_device},
        )

    def place(chunk):
        row = pl.multiple_of((chunk // col_blocks) * 16, 16)
        col = pl.multiple_of((chunk % col_blocks) * chunk_cols, 128)
        return pl.ds(row, 16), pl.ds(col, chunk_cols)

    def write(p, chunk, which, codes_ref):
        row = pl.multiple_of((chunk // col_blocks) * 16 + which * half_rows, 16)
        col = pl.multiple_of((chunk % col_blocks) * chunk_cols + p * columns, 128)
        out_ref[pl.ds(row, 16), pl.ds(col, chunk_cols)] = decode(codes_ref, 16)

    def compute(p):
        start = p * columns
        bricks = volume_buf.reshape(full, width)
        transfer = transfer_ref[:, start % cells : start % cells + columns]
        slices = jnp.dot(
            weight_ref[...], bricks[:, start : start + columns],
            preferred_element_type=jnp.float32,
        )
        tiles = tiles_buf[:, start : start + columns].astype(jnp.float32)
        back = (transfer * (transfer * slices - tiles)).astype(jnp.bfloat16)
        grads_ref[p] = scale * jnp.dot(
            weight_t_ref[...], back, preferred_element_type=jnp.float32
        )
        core_copy(p).start()

    def to_pair(p):
        core_copy(p).wait_recv()
        mine = pl.multiple_of(side * half_rows, 16)
        his = pl.multiple_of((1 - side) * half_rows, 16)
        here = core * owner_rows
        encode(
            grads_ref[p, pl.ds(pl.multiple_of(here + his, 16), half_rows), :]
            + other_ref[p, pl.ds(his, half_rows), :],
            pair_out.at[p],
        )
        pair_copy(p).start()
        half_ref[p] = (
            grads_ref[p, pl.ds(pl.multiple_of(here + mine, 16), half_rows), :]
            + other_ref[p, pl.ds(mine, half_rows), :]
        )

    def scatter(p):
        pair_copy(p).wait_recv()
        half_ref[p] += decode(pair_in.at[p], half_rows)

        def one(step, carry):
            target = peer(step)
            rows, cols = place(target)
            encode(half_ref[p, rows, cols], send_ref.at[p, target])
            rs_copy(p, target, me).start()
            return carry

        lax.fori_loop(1, outer, one, 0)
        rows, cols = place(me)
        total_ref[p] = half_ref[p, rows, cols]

    def collect(p):
        def one(step, carry):
            source = peer(outer - step)
            rs_copy(p, source, source).wait_recv()
            total_ref[p] += decode(recv_ref.at[p, source], 16)
            return carry

        lax.fori_loop(1, outer, one, 0)
        encode(total_ref[p], gather_ref.at[p, me])

        def share(step, carry):
            ag_copy(p, peer(step), me).start()
            return carry

        lax.fori_loop(1, outer, share, 0)
        fw_copy(p, me).start()
        write(p, me, side, gather_ref.at[p, me])

    def forward(p):
        def one(step, carry):
            source = peer(outer - step)
            ag_copy(p, source, source).wait_recv()
            fw_copy(p, source).start()
            write(p, source, side, gather_ref.at[p, source])
            return carry

        lax.fori_loop(1, outer, one, 0)

    def finish(p):
        def one(step, carry):
            source = peer(outer - step)
            fw_copy(p, source).wait_recv()
            write(p, source, 1 - side, pair_gather.at[p, source])
            return carry

        lax.fori_loop(0, outer, one, 0)

    stages = [compute, to_pair, scatter, collect, forward, finish]
    for step in range(pieces + len(stages) - 1):
        for age, stage in enumerate(stages):
            if 0 <= step - age < pieces:
                stage(step - age)

    for p in range(pieces):
        core_copy(p).wait_send()
        pair_copy(p).wait_send()

        def drain(step, carry, p=p):
            target = peer(step)
            rs_copy(p, target, me).wait_send()
            ag_copy(p, target, me).wait_send()
            fw_copy(p, target).wait_send()
            return carry

        lax.fori_loop(1, outer, drain, 0)
        fw_copy(p, me).wait_send()


def on_device(images, pose_index, ctf_index, crossing, volume, pose_table, ctf_table):
    image_count, side, _ = images.shape
    owned, planes, parts, cells = volume.shape
    tile_rows = side // planes
    tile_count = tile_rows * tile_rows
    owners = lax.axis_size("vol")
    peers = lax.axis_size("img")
    bricks = owned * owners
    rows = image_count * tile_count
    width = parts * cells
    weight_rows = bricks * planes
    total_images = image_count * peers * owners
    grad_scale = 2.0 * math.sqrt(planes * bricks / (total_images * tile_count))
    first, second = dft_tables(side, tile_rows)

    chosen = pose_index[:, None] == lax.iota(jnp.int32, pose_table.shape[0])[None, :]
    pose_rows = jnp.einsum(
        "np,ptk->nkt", chosen.astype(jnp.bfloat16), pose_table.astype(jnp.bfloat16),
        preferred_element_type=jnp.bfloat16,
    )
    owner_rows = owned * planes
    half_rows = owner_rows // 2
    outer = peers // 2
    col_blocks = max(1, outer // (half_rows // 16))
    pieces = min(4, width // (128 * col_blocks))
    columns = width // pieces
    chunk = (16, columns // col_blocks)
    code = (pieces, outer, 16 * (chunk[1] // 128) + 16, 128)
    pair_code = (pieces, half_rows * (columns // 128) + 16, 128)
    summed = pl.pallas_call(
        functools.partial(gradient_kernel, grad_scale, pieces, outer, col_blocks),
        out_shape=jax.ShapeDtypeStruct((owner_rows, width), jnp.float32),
        in_specs=[pl.BlockSpec(memory_space=pltpu.SMEM)]
        + [pl.BlockSpec(memory_space=pltpu.VMEM)] * 2
        + [pl.BlockSpec(memory_space=pl.ANY)] * 5,
        out_specs=pl.BlockSpec(memory_space=pltpu.VMEM),
        scratch_shapes=[
            pltpu.VMEM(ctf_table.shape, jnp.float32),
            pltpu.VMEM((owners, owner_rows, width), jnp.bfloat16),
            pltpu.VMEM(images.shape, jnp.bfloat16),
            pltpu.VMEM(first.shape, jnp.bfloat16),
            pltpu.VMEM(second.shape, jnp.bfloat16),
            pltpu.VMEM((rows, width), jnp.bfloat16),
            pltpu.VMEM((rows, weight_rows), jnp.bfloat16),
            pltpu.VMEM((weight_rows, rows), jnp.bfloat16),
            pltpu.VMEM((rows, cells), jnp.float32),
            pltpu.VMEM((pieces, weight_rows, columns), jnp.float32),
            pltpu.VMEM((pieces, owner_rows, columns), jnp.float32),
            pltpu.VMEM(pair_code, jnp.int16),
            pltpu.VMEM(pair_code, jnp.int16),
            pltpu.VMEM((pieces, half_rows, columns), jnp.float32),
            pltpu.VMEM(code, jnp.int16),
            pltpu.VMEM(code, jnp.int16),
            pltpu.VMEM((pieces,) + chunk, jnp.float32),
            pltpu.VMEM(code, jnp.int16),
            pltpu.VMEM(code, jnp.int16),
            pltpu.SemaphoreType.DMA((4,)),
            pltpu.SemaphoreType.DMA((image_count,)),
            pltpu.SemaphoreType.DMA,
            pltpu.SemaphoreType.DMA,
        ]
        + [pltpu.SemaphoreType.DMA((pieces,))] * 4
        + [pltpu.SemaphoreType.DMA((pieces, outer))] * 6,
        compiler_params=pltpu.CompilerParams(
            collective_id=0, has_side_effects=True, vmem_limit_bytes=56 * 2**20
        ),
        cost_estimate=pl.CostEstimate(
            flops=4 * rows * weight_rows * width, bytes_accessed=8 * 2**20, transcendentals=0
        ),
    )(
        ctf_index, crossing, pose_rows, ctf_table, volume.reshape(owner_rows, width),
        images, jnp.asarray(first), jnp.asarray(second),
    )
    return summed.reshape(owned, planes, parts, cells)


def solution(mesh):
    in_specs = (
        P(("parts", "img", "vol"), None, None),
        P(("parts", "img", "vol")),
        P(("parts", "img", "vol")),
        P(("parts", "img", "vol"), None),
        P(("parts", "vol"), None, None, None),
        P(),
        P(),
    )
    out_specs = P(("parts", "vol"), None, None, None)
    return jax.shard_map(
        on_device, mesh=mesh, in_specs=in_specs, out_specs=out_specs, check_vma=False
    )
```

```python
import functools
import math

import jax
import jax.numpy as jnp
import numpy as np
from jax import lax
from jax.experimental import pallas as pl
from jax.experimental.pallas import tpu as pltpu
from jax.sharding import PartitionSpec as P

MESH = pl.DeviceIdType.MESH
LN2 = math.log(2.0)


def dft_tables(side, tile_rows):
    position = np.arange(side, dtype=np.int32)
    product = position[:, None] * position[None, :] % side
    angles = product.astype(np.float32) * np.float32(2.0 * math.pi / side)
    scale = np.float32(1.0 / math.sqrt(side))
    cosine = np.cos(angles) * scale
    sine = np.sin(angles) * scale
    first = np.concatenate([cosine, sine], axis=1)
    order = position.reshape(tile_rows, side // tile_rows).T.reshape(-1)
    cos_rows, sin_rows = cosine[order], sine[order]
    second = np.concatenate(
        [
            np.concatenate([cos_rows, -sin_rows], axis=1),
            np.concatenate([-sin_rows, -cos_rows], axis=1),
        ],
        axis=0,
    )
    return first.astype(jnp.bfloat16), second.astype(jnp.bfloat16)


def block_transpose(parts, lane):
    low = lane < 64
    odd = (lane // 32) % 2 == 1
    x0, x1, x2, x3 = parts
    a0 = jnp.where(low, x0, pltpu.roll(x2, 64, 1))
    a2 = jnp.where(low, pltpu.roll(x0, 64, 1), x2)
    a1 = jnp.where(low, x1, pltpu.roll(x3, 64, 1))
    a3 = jnp.where(low, pltpu.roll(x1, 64, 1), x3)
    y0 = jnp.where(odd, pltpu.roll(a1, 32, 1), a0)
    y1 = jnp.where(odd, a1, pltpu.roll(a0, 96, 1))
    y2 = jnp.where(odd, pltpu.roll(a3, 32, 1), a2)
    y3 = jnp.where(odd, a3, pltpu.roll(a2, 96, 1))
    return y0, y1, y2, y3


def tile_spectrum(image, first, second, tiles_ref, start):
    side = image.shape[1]
    half = jnp.dot(image, first, preferred_element_type=jnp.float32).astype(jnp.bfloat16)
    half = jnp.concatenate([half[:, :side], half[:, side:]], axis=0)
    spec = jnp.dot(second, half, preferred_element_type=jnp.float32)
    groups = spec.shape[0] // 32
    spec = spec.reshape(groups, 4, 8, side)
    lane = lax.broadcasted_iota(jnp.int32, (groups * 8, 128), 1)
    for group in range(side // 128):
        parts = [
            spec[:, low, :, group * 128 : (group + 1) * 128].reshape(groups * 8, 128)
            for low in range(4)
        ]
        done = [y.reshape(groups, 8, 128) for y in block_transpose(parts, lane)]
        for pair in range(2):
            both = jnp.concatenate([done[2 * pair], done[2 * pair + 1]], axis=1)
            both = both.astype(jnp.bfloat16)
            rows = pl.ds(pl.multiple_of(start + group * 32 + pair * 16, 16), 16)
            for g in range(groups):
                tiles_ref[rows, g * 128 : (g + 1) * 128] = both[g]


def encode(values, out_ref):
    height, width = values.shape
    top = jnp.max(jnp.abs(values), axis=1, keepdims=True)
    peak = top[:16]
    for row in range(16, height, 16):
        peak = jnp.maximum(peak, top[row : row + 16])
    exponent = jnp.ceil(jnp.log(jnp.maximum(peak, 1e-30)) * (1.0 / LN2))
    factor = jnp.broadcast_to(jnp.exp((14.0 - exponent) * LN2), (16, 128))
    for col in range(0, width, 128):
        for row in range(0, height, 16):
            block = values[row : row + 16, col : col + 128]
            codes = jnp.floor(block * factor + 0.5).astype(jnp.int32).astype(jnp.int16)
            place = (col // 128) * height + row
            out_ref[place : place + 16, :] = codes
    spread = jnp.broadcast_to(exponent, (16, 128)).astype(jnp.int32).astype(jnp.int16)
    out_ref[height * (width // 128) :, :] = spread


def decode(in_ref, height):
    total = in_ref.shape[0] - 16
    exponent = in_ref[total:, :].astype(jnp.int32).astype(jnp.float32)
    factor = jnp.exp((exponent - 14.0) * LN2)
    columns = []
    for base in range(0, total, height):
        rows = [
            in_ref[base + row : base + row + 16, :].astype(jnp.int32).astype(jnp.float32) * factor
            for row in range(0, height, 16)
        ]
        columns.append(jnp.concatenate(rows, axis=0))
    return jnp.concatenate(columns, axis=1)


def gradient_kernel(
    scale, pieces, outer, col_blocks,
    ctf_index_ref, crossing_ref, pose_rows_ref, ctf_ref, volume_ref, image_ref, first_ref,
    second_ref, out_ref,
    ctf_buf, raw_buf, volume_buf, image_buf, first_buf, second_buf, tiles_buf,
    weight_ref, weight_t_ref, transfer_ref,
    grads_ref, other_ref, pair_out, pair_in, half_ref, send_ref, recv_ref, total_ref,
    gather_ref, pair_gather, load_sem, image_sem, vol_send, vol_recv, core_send, core_recv, pair_send, pair_recv,
    rs_send, rs_recv, ag_send, ag_recv, fw_send, fw_recv,
):
    img = lax.axis_index("img")
    core = lax.axis_index("vol")
    me = img // 2
    side = img - 2 * me
    pair_device = 2 * me + 1 - side
    owner_rows, width = out_ref.shape[0], volume_buf.shape[2]
    half_rows = owner_rows // 2
    cells = transfer_ref.shape[1]
    columns = width // pieces
    chunk_cols = columns // col_blocks

    image_count = image_buf.shape[0]
    own_bricks = volume_buf.at[core]
    loads = [
        pltpu.make_async_copy(source, target, load_sem.at[k])
        for k, (source, target) in enumerate(
            [
                (volume_ref, raw_buf),
                (first_ref, first_buf),
                (second_ref, second_buf),
                (ctf_ref, ctf_buf),
            ]
        )
    ]
    images = [
        pltpu.make_async_copy(image_ref.at[n], image_buf.at[n], image_sem.at[n])
        for n in range(image_count)
    ]
    for load in loads[:3] + images + loads[3:]:
        load.start()

    barrier = pltpu.get_barrier_semaphore()
    pl.semaphore_signal(barrier, inc=1, device_id={"vol": 1 - core}, device_id_type=MESH)
    pl.semaphore_signal(barrier, inc=1, device_id={"img": pair_device}, device_id_type=MESH)

    def peer(step):
        return lax.rem(me + step, outer)

    def greet(step, carry):
        pl.semaphore_signal(
            barrier, inc=1, device_id={"img": 2 * peer(step) + side}, device_id_type=MESH
        )
        return carry

    lax.fori_loop(1, outer, greet, 0)

    planes = pose_rows_ref.shape[1]
    tile_count = pose_rows_ref.shape[2]
    tile_rows = tile_count // 8
    full, row_count = weight_t_ref.shape
    poses = jnp.concatenate(
        [pose_rows_ref[n].astype(jnp.float32) for n in range(image_count)], axis=1
    )
    crossed = jnp.concatenate([crossing_ref[n : n + 1, :] for n in range(image_count)], axis=1)
    brick = lax.broadcasted_iota(jnp.int32, (full, row_count), 0) // planes
    wide = jnp.where(
        brick == crossed, jnp.concatenate([poses] * (full // planes), axis=0), 0.0
    ).astype(jnp.bfloat16)
    column = lax.broadcasted_iota(jnp.int32, (1, row_count), 1)
    source = (
        column // tile_count * tile_count + column % 8 * tile_rows + column % tile_count // 8
    )
    order = jnp.where(
        lax.broadcasted_iota(jnp.int32, (row_count, row_count), 0) == source, 1.0, 0.0
    ).astype(jnp.bfloat16)
    wide = jnp.dot(wide, order, preferred_element_type=jnp.float32)
    weight_t_ref[...] = wide.astype(jnp.bfloat16)
    weight_ref[...] = wide.T.astype(jnp.bfloat16)

    def remote(source, target, send, recv, device):
        return pltpu.make_async_remote_copy(
            src_ref=source, dst_ref=target, send_sem=send, recv_sem=recv,
            device_id=device, device_id_type=MESH,
        )

    volume_copy = remote(
        own_bricks, own_bricks, vol_send, vol_recv, {"vol": 1 - core}
    )
    loads[0].wait()
    for part in range(raw_buf.shape[1]):
        own_bricks[:, part * cells : (part + 1) * cells] = raw_buf[:, part, :]
    pl.semaphore_wait(barrier, outer + 1)
    volume_copy.start()
    loads[1].wait()
    loads[2].wait()
    for n in range(image_count):
        images[n].wait()

    def transform(n, carry):
        start = n * tile_count
        tile_spectrum(image_buf[n], first_buf[...], second_buf[...], tiles_buf, start)
        return carry

    lax.fori_loop(0, image_count, transform, 0, unroll=4)
    loads[3].wait()
    for n in range(image_count):
        rows = ctf_buf[ctf_index_ref[n]].reshape(tile_rows, 8, cells)
        transfer_ref[n * tile_count : (n + 1) * tile_count, :] = jnp.swapaxes(
            rows, 0, 1
        ).reshape(tile_count, cells)
    volume_copy.wait()

    def core_copy(p):
        there = pl.multiple_of((1 - core) * owner_rows, 16)
        return remote(
            grads_ref.at[p, pl.ds(there, owner_rows), :], other_ref.at[p],
            core_send.at[p], core_recv.at[p], {"vol": 1 - core},
        )

    def pair_copy(p):
        return remote(
            pair_out.at[p], pair_in.at[p], pair_send.at[p], pair_recv.at[p],
            {"img": pair_device},
        )

    def rs_copy(p, target, slot):
        return remote(
            send_ref.at[p, target], recv_ref.at[p, slot],
            rs_send.at[p, target], rs_recv.at[p, slot], {"img": 2 * target + side},
        )

    def ag_copy(p, target, slot):
        return remote(
            gather_ref.at[p, slot], gather_ref.at[p, slot],
            ag_send.at[p, target], ag_recv.at[p, slot], {"img": 2 * target + side},
        )

    def fw_copy(p, slot):
        return remote(
            gather_ref.at[p, slot], pair_gather.at[p, slot],
            fw_send.at[p, slot], fw_recv.at[p, slot], {"img": pair_device},
        )

    def place(chunk):
        row = pl.multiple_of((chunk // col_blocks) * 16, 16)
        col = pl.multiple_of((chunk % col_blocks) * chunk_cols, 128)
        return pl.ds(row, 16), pl.ds(col, chunk_cols)

    def write(p, chunk, which, codes_ref):
        row = pl.multiple_of((chunk // col_blocks) * 16 + which * half_rows, 16)
        part, start = divmod(p * columns, cells)
        col = pl.multiple_of((chunk % col_blocks) * chunk_cols + start, 128)
        out_ref[pl.ds(row, 16), part, pl.ds(col, chunk_cols)] = decode(codes_ref, 16)

    def compute(p):
        start = p * columns
        bricks = volume_buf.reshape(full, width)
        transfer = transfer_ref[:, start % cells : start % cells + columns]
        slices = jnp.dot(
            weight_ref[...], bricks[:, start : start + columns],
            preferred_element_type=jnp.float32,
        )
        tiles = tiles_buf[:, start : start + columns].astype(jnp.float32)
        back = (transfer * (transfer * slices - tiles)).astype(jnp.bfloat16)
        grads_ref[p] = scale * jnp.dot(
            weight_t_ref[...], back, preferred_element_type=jnp.float32
        )
        core_copy(p).start()

    def to_pair(p):
        core_copy(p).wait_recv()
        mine = pl.multiple_of(side * half_rows, 16)
        his = pl.multiple_of((1 - side) * half_rows, 16)
        here = core * owner_rows
        encode(
            grads_ref[p, pl.ds(pl.multiple_of(here + his, 16), half_rows), :]
            + other_ref[p, pl.ds(his, half_rows), :],
            pair_out.at[p],
        )
        pair_copy(p).start()
        half_ref[p] = (
            grads_ref[p, pl.ds(pl.multiple_of(here + mine, 16), half_rows), :]
            + other_ref[p, pl.ds(mine, half_rows), :]
        )

    def scatter(p):
        pair_copy(p).wait_recv()
        half_ref[p] += decode(pair_in.at[p], half_rows)

        def one(step, carry):
            target = peer(step)
            rows, cols = place(target)
            encode(half_ref[p, rows, cols], send_ref.at[p, target])
            rs_copy(p, target, me).start()
            return carry

        lax.fori_loop(1, outer, one, 0)
        rows, cols = place(me)
        total_ref[p] = half_ref[p, rows, cols]

    def collect(p):
        def one(step, carry):
            source = peer(outer - step)
            rs_copy(p, source, source).wait_recv()
            total_ref[p] += decode(recv_ref.at[p, source], 16)
            return carry

        lax.fori_loop(1, outer, one, 0)
        encode(total_ref[p], gather_ref.at[p, me])

        def share(step, carry):
            ag_copy(p, peer(step), me).start()
            return carry

        lax.fori_loop(1, outer, share, 0)
        fw_copy(p, me).start()
        write(p, me, side, gather_ref.at[p, me])

    def forward(p):
        def one(step, carry):
            source = peer(outer - step)
            ag_copy(p, source, source).wait_recv()
            fw_copy(p, source).start()
            write(p, source, side, gather_ref.at[p, source])
            return carry

        lax.fori_loop(1, outer, one, 0)

    def finish(p):
        def one(step, carry):
            source = peer(outer - step)
            fw_copy(p, source).wait_recv()
            write(p, source, 1 - side, pair_gather.at[p, source])
            return carry

        lax.fori_loop(0, outer, one, 0)

    stages = [compute, to_pair, scatter, collect, forward, finish]
    for step in range(pieces + len(stages) - 1):
        for age, stage in enumerate(stages):
            if 0 <= step - age < pieces:
                stage(step - age)

    for p in range(pieces):
        core_copy(p).wait_send()
        pair_copy(p).wait_send()

        def drain(step, carry, p=p):
            target = peer(step)
            rs_copy(p, target, me).wait_send()
            ag_copy(p, target, me).wait_send()
            fw_copy(p, target).wait_send()
            return carry

        lax.fori_loop(1, outer, drain, 0)
        fw_copy(p, me).wait_send()


def on_device(images, pose_index, ctf_index, crossing, volume, pose_table, ctf_table):
    image_count, side, _ = images.shape
    owned, planes, parts, cells = volume.shape
    tile_rows = side // planes
    tile_count = tile_rows * tile_rows
    owners = lax.axis_size("vol")
    peers = lax.axis_size("img")
    bricks = owned * owners
    rows = image_count * tile_count
    width = parts * cells
    weight_rows = bricks * planes
    total_images = image_count * peers * owners
    grad_scale = 2.0 * math.sqrt(planes * bricks / (total_images * tile_count))
    first, second = dft_tables(side, tile_rows)

    chosen = pose_index[:, None] == lax.iota(jnp.int32, pose_table.shape[0])[None, :]
    pose_rows = jnp.einsum(
        "np,ptk->nkt", chosen.astype(jnp.bfloat16), pose_table.astype(jnp.bfloat16),
        preferred_element_type=jnp.bfloat16,
    )
    owner_rows = owned * planes
    half_rows = owner_rows // 2
    outer = peers // 2
    col_blocks = max(1, outer // (half_rows // 16))
    pieces = min(2, width // (128 * col_blocks))
    columns = width // pieces
    chunk = (16, columns // col_blocks)
    code = (pieces, outer, 16 * (chunk[1] // 128) + 16, 128)
    pair_code = (pieces, half_rows * (columns // 128) + 16, 128)
    summed = pl.pallas_call(
        functools.partial(gradient_kernel, grad_scale, pieces, outer, col_blocks),
        out_shape=jax.ShapeDtypeStruct((owner_rows, parts, cells), jnp.float32),
        in_specs=[pl.BlockSpec(memory_space=pltpu.SMEM)]
        + [pl.BlockSpec(memory_space=pltpu.VMEM)] * 2
        + [pl.BlockSpec(memory_space=pl.ANY)] * 5,
        out_specs=pl.BlockSpec(memory_space=pltpu.VMEM),
        scratch_shapes=[
            pltpu.VMEM(ctf_table.shape, jnp.float32),
            pltpu.VMEM((owner_rows, parts, cells), jnp.bfloat16),
            pltpu.VMEM((owners, owner_rows, width), jnp.bfloat16),
            pltpu.VMEM(images.shape, jnp.bfloat16),
            pltpu.VMEM(first.shape, jnp.bfloat16),
            pltpu.VMEM(second.shape, jnp.bfloat16),
            pltpu.VMEM((rows, width), jnp.bfloat16),
            pltpu.VMEM((rows, weight_rows), jnp.bfloat16),
            pltpu.VMEM((weight_rows, rows), jnp.bfloat16),
            pltpu.VMEM((rows, cells), jnp.float32),
            pltpu.VMEM((pieces, weight_rows, columns), jnp.float32),
            pltpu.VMEM((pieces, owner_rows, columns), jnp.float32),
            pltpu.VMEM(pair_code, jnp.int16),
            pltpu.VMEM(pair_code, jnp.int16),
            pltpu.VMEM((pieces, half_rows, columns), jnp.float32),
            pltpu.VMEM(code, jnp.int16),
            pltpu.VMEM(code, jnp.int16),
            pltpu.VMEM((pieces,) + chunk, jnp.float32),
            pltpu.VMEM(code, jnp.int16),
            pltpu.VMEM(code, jnp.int16),
            pltpu.SemaphoreType.DMA((4,)),
            pltpu.SemaphoreType.DMA((image_count,)),
            pltpu.SemaphoreType.DMA,
            pltpu.SemaphoreType.DMA,
        ]
        + [pltpu.SemaphoreType.DMA((pieces,))] * 4
        + [pltpu.SemaphoreType.DMA((pieces, outer))] * 6,
        compiler_params=pltpu.CompilerParams(
            collective_id=0, has_side_effects=True, vmem_limit_bytes=56 * 2**20
        ),
        cost_estimate=pl.CostEstimate(
            flops=4 * rows * weight_rows * width, bytes_accessed=8 * 2**20, transcendentals=0
        ),
    )(
        ctf_index, crossing, pose_rows, ctf_table, volume.reshape(owner_rows, parts, cells),
        images, jnp.asarray(first), jnp.asarray(second),
    )
    return summed.reshape(owned, planes, parts, cells)


def solution(mesh):
    in_specs = (
        P(("parts", "img", "vol"), None, None),
        P(("parts", "img", "vol")),
        P(("parts", "img", "vol")),
        P(("parts", "img", "vol"), None),
        P(("parts", "vol"), None, None, None),
        P(),
        P(),
    )
    out_specs = P(("parts", "vol"), None, None, None)
    return jax.shard_map(
        on_device, mesh=mesh, in_specs=in_specs, out_specs=out_specs, check_vma=False
    )
```

```python
import functools
import math

import jax
import jax.numpy as jnp
import numpy as np
from jax import lax
from jax.experimental import pallas as pl
from jax.experimental.pallas import tpu as pltpu
from jax.sharding import PartitionSpec as P

MESH = pl.DeviceIdType.MESH
LN2 = math.log(2.0)


def dft_tables(side, tile_rows):
    position = np.arange(side, dtype=np.int32)
    product = position[:, None] * position[None, :] % side
    angles = product.astype(np.float32) * np.float32(2.0 * math.pi / side)
    scale = np.float32(1.0 / math.sqrt(side))
    cosine = np.cos(angles) * scale
    sine = np.sin(angles) * scale
    first = np.concatenate([cosine, sine], axis=1)
    order = position.reshape(tile_rows, side // tile_rows).T.reshape(-1)
    cos_rows, sin_rows = cosine[order], sine[order]
    second = np.concatenate(
        [
            np.concatenate([cos_rows, -sin_rows], axis=1),
            np.concatenate([-sin_rows, -cos_rows], axis=1),
        ],
        axis=0,
    )
    return first.astype(jnp.bfloat16), second.astype(jnp.bfloat16)


def block_transpose(parts, lane):
    low = lane < 64
    odd = (lane // 32) % 2 == 1
    x0, x1, x2, x3 = parts
    a0 = jnp.where(low, x0, pltpu.roll(x2, 64, 1))
    a2 = jnp.where(low, pltpu.roll(x0, 64, 1), x2)
    a1 = jnp.where(low, x1, pltpu.roll(x3, 64, 1))
    a3 = jnp.where(low, pltpu.roll(x1, 64, 1), x3)
    y0 = jnp.where(odd, pltpu.roll(a1, 32, 1), a0)
    y1 = jnp.where(odd, a1, pltpu.roll(a0, 96, 1))
    y2 = jnp.where(odd, pltpu.roll(a3, 32, 1), a2)
    y3 = jnp.where(odd, a3, pltpu.roll(a2, 96, 1))
    return y0, y1, y2, y3


def tile_spectrum(image, first, second, tiles_ref, start):
    side = image.shape[1]
    half = jnp.dot(image, first, preferred_element_type=jnp.float32).astype(jnp.bfloat16)
    half = jnp.concatenate([half[:, :side], half[:, side:]], axis=0)
    spec = jnp.dot(second, half, preferred_element_type=jnp.float32)
    groups = spec.shape[0] // 32
    spec = spec.reshape(groups, 4, 8, side)
    lane = lax.broadcasted_iota(jnp.int32, (groups * 8, 128), 1)
    for group in range(side // 128):
        parts = [
            spec[:, low, :, group * 128 : (group + 1) * 128].reshape(groups * 8, 128)
            for low in range(4)
        ]
        done = [y.reshape(groups, 8, 128) for y in block_transpose(parts, lane)]
        for pair in range(2):
            both = jnp.concatenate([done[2 * pair], done[2 * pair + 1]], axis=1)
            both = both.astype(jnp.bfloat16)
            rows = pl.ds(pl.multiple_of(start + group * 32 + pair * 16, 16), 16)
            for g in range(groups):
                tiles_ref[rows, g * 128 : (g + 1) * 128] = both[g]


def encode(values, out_ref):
    height, width = values.shape
    top = jnp.max(jnp.abs(values), axis=1, keepdims=True)
    peak = top[:16]
    for row in range(16, height, 16):
        peak = jnp.maximum(peak, top[row : row + 16])
    exponent = jnp.ceil(jnp.log(jnp.maximum(peak, 1e-30)) * (1.0 / LN2))
    factor = jnp.broadcast_to(jnp.exp((14.0 - exponent) * LN2), (16, 128))
    for col in range(0, width, 128):
        for row in range(0, height, 16):
            block = values[row : row + 16, col : col + 128]
            codes = jnp.floor(block * factor + 0.5).astype(jnp.int32).astype(jnp.int16)
            place = (col // 128) * height + row
            out_ref[place : place + 16, :] = codes
    spread = jnp.broadcast_to(exponent, (16, 128)).astype(jnp.int32).astype(jnp.int16)
    out_ref[height * (width // 128) :, :] = spread


def decode(in_ref, height):
    total = in_ref.shape[0] - 16
    exponent = in_ref[total:, :].astype(jnp.int32).astype(jnp.float32)
    factor = jnp.exp((exponent - 14.0) * LN2)
    columns = []
    for base in range(0, total, height):
        rows = [
            in_ref[base + row : base + row + 16, :].astype(jnp.int32).astype(jnp.float32) * factor
            for row in range(0, height, 16)
        ]
        columns.append(jnp.concatenate(rows, axis=0))
    return jnp.concatenate(columns, axis=1)


def gradient_kernel(
    scale, pieces, outer, col_blocks,
    ctf_index_ref, crossing_ref, pose_rows_ref, ctf_ref, volume_ref, image_ref, first_ref,
    second_ref, out_ref,
    ctf_buf, raw_buf, volume_buf, image_buf, first_buf, second_buf, tiles_buf,
    weight_ref, weight_t_ref, transfer_ref,
    grads_ref, other_ref, pair_out, pair_in, half_ref, send_ref, recv_ref, total_ref,
    gather_ref, pair_gather, load_sem, image_sem, vol_send, vol_recv, core_send, core_recv, pair_send, pair_recv,
    rs_send, rs_recv, ag_send, ag_recv, fw_send, fw_recv,
):
    img = lax.axis_index("img")
    core = lax.axis_index("vol")
    me = img // 2
    side = img - 2 * me
    pair_device = 2 * me + 1 - side
    owner_rows, width = out_ref.shape[0], volume_buf.shape[2]
    half_rows = owner_rows // 2
    cells = transfer_ref.shape[1]
    columns = width // pieces
    chunk_cols = columns // col_blocks

    image_count = image_buf.shape[0]
    own_bricks = volume_buf.at[core]
    loads = [
        pltpu.make_async_copy(source, target, load_sem.at[k])
        for k, (source, target) in enumerate(
            [
                (volume_ref, raw_buf),
                (first_ref, first_buf),
                (second_ref, second_buf),
                (ctf_ref, ctf_buf),
            ]
        )
    ]
    images = [
        pltpu.make_async_copy(image_ref.at[n], image_buf.at[n], image_sem.at[n])
        for n in range(image_count)
    ]
    for load in loads[:3] + images + loads[3:]:
        load.start()

    barrier = pltpu.get_barrier_semaphore()
    pl.semaphore_signal(barrier, inc=1, device_id={"vol": 1 - core}, device_id_type=MESH)
    pl.semaphore_signal(barrier, inc=1, device_id={"img": pair_device}, device_id_type=MESH)

    def peer(step):
        return lax.rem(me + step, outer)

    def greet(step, carry):
        pl.semaphore_signal(
            barrier, inc=1, device_id={"img": 2 * peer(step) + side}, device_id_type=MESH
        )
        return carry

    lax.fori_loop(1, outer, greet, 0)

    planes = pose_rows_ref.shape[0]
    tile_count = pose_rows_ref.shape[2]
    tile_rows = tile_count // 8
    full, row_count = weight_t_ref.shape
    poses = jnp.concatenate(
        [pose_rows_ref[:, n, :] for n in range(image_count)], axis=1
    )
    crossed = jnp.concatenate([crossing_ref[n : n + 1, :] for n in range(image_count)], axis=1)
    brick = lax.broadcasted_iota(jnp.int32, (full, row_count), 0) // planes
    wide = jnp.where(
        brick == crossed, jnp.concatenate([poses] * (full // planes), axis=0), 0.0
    ).astype(jnp.bfloat16)
    column = lax.broadcasted_iota(jnp.int32, (1, row_count), 1)
    source = (
        column // tile_count * tile_count + column % 8 * tile_rows + column % tile_count // 8
    )
    order = jnp.where(
        lax.broadcasted_iota(jnp.int32, (row_count, row_count), 0) == source, 1.0, 0.0
    ).astype(jnp.bfloat16)
    wide = jnp.dot(wide, order, preferred_element_type=jnp.float32)
    weight_t_ref[...] = wide.astype(jnp.bfloat16)
    weight_ref[...] = wide.T.astype(jnp.bfloat16)

    def remote(source, target, send, recv, device):
        return pltpu.make_async_remote_copy(
            src_ref=source, dst_ref=target, send_sem=send, recv_sem=recv,
            device_id=device, device_id_type=MESH,
        )

    volume_copy = remote(
        own_bricks, own_bricks, vol_send, vol_recv, {"vol": 1 - core}
    )
    loads[0].wait()
    for part in range(raw_buf.shape[1]):
        own_bricks[:, part * cells : (part + 1) * cells] = raw_buf[:, part, :]
    pl.semaphore_wait(barrier, outer + 1)
    volume_copy.start()
    loads[1].wait()
    loads[2].wait()
    for n in range(image_count):
        images[n].wait()

    def transform(n, carry):
        start = n * tile_count
        tile_spectrum(image_buf[n], first_buf[...], second_buf[...], tiles_buf, start)
        return carry

    lax.fori_loop(0, image_count, transform, 0, unroll=8)
    loads[3].wait()
    for n in range(image_count):
        rows = ctf_buf[ctf_index_ref[n]].reshape(tile_rows, 8, cells)
        transfer_ref[n * tile_count : (n + 1) * tile_count, :] = jnp.swapaxes(
            rows, 0, 1
        ).reshape(tile_count, cells)
    volume_copy.wait()

    def core_copy(p):
        there = pl.multiple_of((1 - core) * owner_rows, 16)
        return remote(
            grads_ref.at[p, pl.ds(there, owner_rows), :], other_ref.at[p],
            core_send.at[p], core_recv.at[p], {"vol": 1 - core},
        )

    def pair_copy(p):
        return remote(
            pair_out.at[p], pair_in.at[p], pair_send.at[p], pair_recv.at[p],
            {"img": pair_device},
        )

    def rs_copy(p, target, slot):
        return remote(
            send_ref.at[p, target], recv_ref.at[p, slot],
            rs_send.at[p, target], rs_recv.at[p, slot], {"img": 2 * target + side},
        )

    def ag_copy(p, target, slot):
        return remote(
            gather_ref.at[p, slot], gather_ref.at[p, slot],
            ag_send.at[p, target], ag_recv.at[p, slot], {"img": 2 * target + side},
        )

    def fw_copy(p, slot):
        return remote(
            gather_ref.at[p, slot], pair_gather.at[p, slot],
            fw_send.at[p, slot], fw_recv.at[p, slot], {"img": pair_device},
        )

    def place(chunk):
        row = pl.multiple_of((chunk // col_blocks) * 16, 16)
        col = pl.multiple_of((chunk % col_blocks) * chunk_cols, 128)
        return pl.ds(row, 16), pl.ds(col, chunk_cols)

    def write(p, chunk, which, codes_ref):
        row = pl.multiple_of((chunk // col_blocks) * 16 + which * half_rows, 16)
        part, start = divmod(p * columns, cells)
        col = pl.multiple_of((chunk % col_blocks) * chunk_cols + start, 128)
        out_ref[pl.ds(row, 16), part, pl.ds(col, chunk_cols)] = decode(codes_ref, 16)

    def compute(p, low, high):
        bricks = volume_buf.reshape(full, width)
        there = pl.ds(pl.multiple_of((1 - core) * owner_rows, 16), owner_rows)
        here = pl.ds(pl.multiple_of(core * owner_rows, 16), owner_rows)
        for col in range(low, high, 256):
            start = p * columns + col
            transfer = transfer_ref[:, start % cells : start % cells + 256]
            slices = jnp.dot(
                weight_ref[...], bricks[:, start : start + 256],
                preferred_element_type=jnp.float32,
            )
            tiles = tiles_buf[:, start : start + 256].astype(jnp.float32)
            back = (transfer * (transfer * slices - tiles)).astype(jnp.bfloat16)
            for rows in (there, here):
                grads_ref[p, rows, col : col + 256] = scale * jnp.dot(
                    weight_t_ref[rows, :], back, preferred_element_type=jnp.float32
                )
        if high == columns:
            core_copy(p).start()

    def to_pair(p):
        core_copy(p).wait_recv()
        mine = pl.multiple_of(side * half_rows, 16)
        his = pl.multiple_of((1 - side) * half_rows, 16)
        here = core * owner_rows
        encode(
            grads_ref[p, pl.ds(pl.multiple_of(here + his, 16), half_rows), :]
            + other_ref[p, pl.ds(his, half_rows), :],
            pair_out.at[p],
        )
        pair_copy(p).start()
        half_ref[p] = (
            grads_ref[p, pl.ds(pl.multiple_of(here + mine, 16), half_rows), :]
            + other_ref[p, pl.ds(mine, half_rows), :]
        )

    def scatter(p):
        pair_copy(p).wait_recv()
        half_ref[p] += decode(pair_in.at[p], half_rows)

        def one(step, carry):
            target = peer(step)
            rows, cols = place(target)
            encode(half_ref[p, rows, cols], send_ref.at[p, target])
            rs_copy(p, target, me).start()
            return carry

        lax.fori_loop(1, outer, one, 0)
        rows, cols = place(me)
        total_ref[p] = half_ref[p, rows, cols]

    def collect(p):
        def one(step, carry):
            source = peer(outer - step)
            rs_copy(p, source, source).wait_recv()
            total_ref[p] += decode(recv_ref.at[p, source], 16)
            return carry

        lax.fori_loop(1, outer, one, 0)
        encode(total_ref[p], gather_ref.at[p, me])

        def share(step, carry):
            ag_copy(p, peer(step), me).start()
            return carry

        lax.fori_loop(1, outer, share, 0)
        fw_copy(p, me).start()
        write(p, me, side, gather_ref.at[p, me])

    def forward(p):
        def one(step, carry):
            source = peer(outer - step)
            ag_copy(p, source, source).wait_recv()
            fw_copy(p, source).start()
            write(p, source, side, gather_ref.at[p, source])
            return carry

        lax.fori_loop(1, outer, one, 0)

    def finish(p):
        def one(step, carry):
            source = peer(outer - step)
            fw_copy(p, source).wait_recv()
            write(p, source, 1 - side, pair_gather.at[p, source])
            return carry

        lax.fori_loop(0, outer, one, 0)

    stages = [to_pair, scatter, collect, forward, finish]
    for step in range(pieces + len(stages)):
        if 0 < step < pieces:
            compute(step, 0, columns // 2)
            to_pair(step - 1)
            compute(step, columns // 2, columns)
        elif step == 0:
            compute(step, 0, columns)
        for age, stage in enumerate(stages, 1):
            if 0 <= step - age < pieces and (age > 1 or step == pieces):
                stage(step - age)

    for p in range(pieces):
        core_copy(p).wait_send()
        pair_copy(p).wait_send()

        def drain(step, carry, p=p):
            target = peer(step)
            rs_copy(p, target, me).wait_send()
            ag_copy(p, target, me).wait_send()
            fw_copy(p, target).wait_send()
            return carry

        lax.fori_loop(1, outer, drain, 0)
        fw_copy(p, me).wait_send()


def on_device(images, pose_index, ctf_index, crossing, volume, pose_table, ctf_table):
    image_count, side, _ = images.shape
    owned, planes, parts, cells = volume.shape
    tile_rows = side // planes
    tile_count = tile_rows * tile_rows
    owners = lax.axis_size("vol")
    peers = lax.axis_size("img")
    bricks = owned * owners
    rows = image_count * tile_count
    width = parts * cells
    weight_rows = bricks * planes
    total_images = image_count * peers * owners
    grad_scale = 2.0 * math.sqrt(planes * bricks / (total_images * tile_count))
    first, second = dft_tables(side, tile_rows)

    chosen = pose_index[:, None] == lax.iota(jnp.int32, pose_table.shape[0])[None, :]
    pose_rows = jnp.einsum(
        "np,ptk->knt", chosen.astype(jnp.float32), pose_table,
        preferred_element_type=jnp.float32,
    )
    owner_rows = owned * planes
    half_rows = owner_rows // 2
    outer = peers // 2
    col_blocks = max(1, outer // (half_rows // 16))
    pieces = min(2, width // (128 * col_blocks))
    columns = width // pieces
    chunk = (16, columns // col_blocks)
    code = (pieces, outer, 16 * (chunk[1] // 128) + 16, 128)
    pair_code = (pieces, half_rows * (columns // 128) + 16, 128)
    summed = pl.pallas_call(
        functools.partial(gradient_kernel, grad_scale, pieces, outer, col_blocks),
        out_shape=jax.ShapeDtypeStruct((owner_rows, parts, cells), jnp.float32),
        in_specs=[pl.BlockSpec(memory_space=pltpu.SMEM)]
        + [pl.BlockSpec(memory_space=pltpu.VMEM)] * 2
        + [pl.BlockSpec(memory_space=pl.ANY)] * 5,
        out_specs=pl.BlockSpec(memory_space=pltpu.VMEM),
        scratch_shapes=[
            pltpu.VMEM(ctf_table.shape, jnp.float32),
            pltpu.VMEM((owner_rows, parts, cells), jnp.bfloat16),
            pltpu.VMEM((owners, owner_rows, width), jnp.bfloat16),
            pltpu.VMEM(images.shape, jnp.bfloat16),
            pltpu.VMEM(first.shape, jnp.bfloat16),
            pltpu.VMEM(second.shape, jnp.bfloat16),
            pltpu.VMEM((rows, width), jnp.bfloat16),
            pltpu.VMEM((rows, weight_rows), jnp.bfloat16),
            pltpu.VMEM((weight_rows, rows), jnp.bfloat16),
            pltpu.VMEM((rows, cells), jnp.float32),
            pltpu.VMEM((pieces, weight_rows, columns), jnp.float32),
            pltpu.VMEM((pieces, owner_rows, columns), jnp.float32),
            pltpu.VMEM(pair_code, jnp.int16),
            pltpu.VMEM(pair_code, jnp.int16),
            pltpu.VMEM((pieces, half_rows, columns), jnp.float32),
            pltpu.VMEM(code, jnp.int16),
            pltpu.VMEM(code, jnp.int16),
            pltpu.VMEM((pieces,) + chunk, jnp.float32),
            pltpu.VMEM(code, jnp.int16),
            pltpu.VMEM(code, jnp.int16),
            pltpu.SemaphoreType.DMA((4,)),
            pltpu.SemaphoreType.DMA((image_count,)),
            pltpu.SemaphoreType.DMA,
            pltpu.SemaphoreType.DMA,
        ]
        + [pltpu.SemaphoreType.DMA((pieces,))] * 4
        + [pltpu.SemaphoreType.DMA((pieces, outer))] * 6,
        compiler_params=pltpu.CompilerParams(
            collective_id=0, has_side_effects=True, vmem_limit_bytes=56 * 2**20
        ),
        cost_estimate=pl.CostEstimate(
            flops=4 * rows * weight_rows * width, bytes_accessed=8 * 2**20, transcendentals=0
        ),
    )(
        ctf_index, crossing, pose_rows, ctf_table, volume.reshape(owner_rows, parts, cells),
        images, jnp.asarray(first), jnp.asarray(second),
    )
    return summed.reshape(owned, planes, parts, cells)


def solution(mesh):
    in_specs = (
        P(("parts", "img", "vol"), None, None),
        P(("parts", "img", "vol")),
        P(("parts", "img", "vol")),
        P(("parts", "img", "vol"), None),
        P(("parts", "vol"), None, None, None),
        P(),
        P(),
    )
    out_specs = P(("parts", "vol"), None, None, None)
    return jax.shard_map(
        on_device, mesh=mesh, in_specs=in_specs, out_specs=out_specs, check_vma=False
    )
```
